32 devices in a mesh: grp: 2 (over x), blk: 16 (over z, y, core).
Axes of the slice: x: 2, y: 2, z: 4, core: 2. Of those that a mesh axis runs over, the one named last changes fastest.
Arguments:
- doc_grads: float32 [24576, 2048], P(('grp', 'blk')), parts along dimension 0, may hold values from -250 to 250
- test_grads: float32 [512, 2048], P(('grp', 'blk')), parts along dimension 0, may hold values from -6 to 6
- eigen_basis: bfloat16 [2, 1024, 1024], replicated, may hold values from -0.1875 to 0.1875
- eigen_values: float32 [2, 1024], replicated, may hold values from 0.01 to 10
Outputs:
- influence: float32 [256, 24576], P(None, ('grp', 'blk')), parts along dimension 1
The draws below stay inside these ranges and needn't reach their ends.
There are 2 independent parts, one for each index of `grp`. The reference program is written for one: setup_inputs(seed, part) draws one part's arguments, and reference() takes and returns one part's arrays. A program takes and returns all parts, laid end to end along the dimension named above; an argument that names none is the same for every part. Nothing has to cross between parts.
All inputs are finite; a program needn't handle non-finite values.
Results may differ from the reference program's by a relative error of at most 0.0029.
Values may be sent and summed in bfloat16 or wider, within the bound.
A program may use at most 128 MiB of HBM per device.

```python
import math
import jax
import jax.numpy as jnp
from jax import lax

K = 1024
LAYERS = 2
DOCS = 12288
QUERIES = 256


def draw_doc_grads(key, part):
    key = jax.random.fold_in(key, 7)
    first, second = jax.random.split(key, 2)
    width = LAYERS * K
    place = jnp.arange(DOCS, dtype=jnp.float32) / DOCS
    rows = jnp.exp(jax.random.uniform(second, (DOCS, 1), minval=0.0, maxval=jnp.log(10.0)))
    base = jax.random.truncated_normal(first, -4.0, 4.0, (DOCS, width))
    rise = jnp.exp(jnp.log(3.0) * place)
    return (base * rise[:, None] * rows).astype(jnp.float32)


def levels(rng, dims, shards, smallest, top_value):
    loudness = 1.0
    for axis_at, shards_of in shards:
        steps = jax.random.uniform(jax.random.fold_in(jax.random.fold_in(rng, 6), axis_at), (shards_of,), jnp.float32, smallest / len(shards), top_value / len(shards))
        loudness = loudness * jnp.repeat(jnp.exp(steps), dims[axis_at] // shards_of).reshape((-1,) + (1,) * (len(dims) - 1 - axis_at))
    return loudness


def scatter_about(rng, shape, scale, bound, cuts=(), kind=jnp.bfloat16):
    gain = levels(rng, shape, cuts, -0.22, 0.18) if cuts else 1.0
    result = jax.random.normal(rng, shape, jnp.float32) * scale * gain
    return jnp.minimum(jnp.maximum(result, -bound), bound).astype(kind)


def setup_inputs(seed: int = 0, part: int = 0) -> dict:
    key_of = jax.random.split(jax.random.key(seed), 5)
    own_keys = jax.random.split(jax.random.fold_in(key_of[4], part), 5)
    doc_grads = draw_doc_grads(jax.random.fold_in(jax.random.fold_in(key_of[4], part), 71), part)
    test_grads = scatter_about(own_keys[1], (QUERIES, LAYERS * K), 1.0, 6.0, ((0, 16),), jnp.float32)
    eigen_basis = scatter_about(key_of[2], (LAYERS, K, K), K ** -0.5, 0.1875)
    eigen_values = jnp.clip(jnp.exp(jax.random.uniform(key_of[3], (LAYERS, K), jnp.float32, math.log(0.01), math.log(10.0))), 0.01, 10.0)
    return {"doc_grads": doc_grads, "test_grads": test_grads, "eigen_basis": eigen_basis, "eigen_values": eigen_values}


def precondition(rows, eigen_basis, eigen_values):
    blocks = []
    for layer in range(LAYERS):
        part = rows[:, layer * K:(layer + 1) * K]
        basis = eigen_basis[layer].astype(jnp.float32)
        values = eigen_values[layer]
        damping = 0.1 * jnp.mean(values)
        rotated = jnp.dot(part, basis, precision=lax.Precision.HIGHEST, preferred_element_type=jnp.float32)
        rotated = rotated / (values + damping)
        blocks.append(lax.dot_general(rotated, basis, (((1,), (1,)), ((), ())), precision=lax.Precision.HIGHEST, preferred_element_type=jnp.float32))
    return jnp.concatenate(blocks, axis=1).astype(jnp.bfloat16)

def reference(doc_grads, test_grads, eigen_basis, eigen_values):
    precond = precondition(test_grads, eigen_basis, eigen_values)
    raw = lax.dot_general(precond.astype(jnp.float32), doc_grads, (((1,), (1,)), ((), ())), precision=lax.Precision.HIGHEST, preferred_element_type=jnp.float32)
    spread = lax.optimization_barrier(jnp.mean(raw * raw, axis=1, keepdims=True))
    return raw / jnp.sqrt(spread + 1e-06)
```

```python
import functools

import jax
import jax.numpy as jnp
from jax import lax
from jax.experimental import pallas as pl
from jax.experimental.pallas import tpu as pltpu
from jax.sharding import PartitionSpec as P

PIECES = 2
TILE = 256
MESH = pl.DeviceIdType.MESH
NT = (((1,), (1,)), ((), ()))


def repeat(count, body):
    if count <= 4:
        for i in range(count):
            body(i)
    else:
        lax.fori_loop(0, count, lambda i, c: (body(i), c)[1], 0)


def split3(x):
    high = x.astype(jnp.bfloat16)
    rest = x - high.astype(jnp.float32)
    mid = rest.astype(jnp.bfloat16)
    low = (rest - mid.astype(jnp.float32)).astype(jnp.bfloat16)
    return jnp.concatenate([high, mid, low], axis=0)


def kernel(
    far, near, docs_hbm, tests_hbm, basis_hbm, values_hbm, out_hbm,
    docs, tests, basis, values, ready, acc, sums,
    docs_sem, tests_sem, basis_sem, values_sem, out_sem,
    send_sem, recv_sem, sums_send, sums_recv,
):
    n = far * near * 2
    layers, width = values.shape
    chunks, _, rows, part = ready.shape
    total_docs = n * docs.shape[1]
    queries = n * rows
    me = lax.axis_index("blk")
    c = lax.rem(me, 2)
    b = lax.rem(me // 2, near)
    a = me // (2 * near)

    def index(a_, b_, c_):
        return (a_ * near + b_) * 2 + c_

    local = []
    tests_in = pltpu.make_async_copy(tests_hbm, tests, tests_sem)
    values_in = pltpu.make_async_copy(values_hbm, values, values_sem)
    basis_in = [
        pltpu.make_async_copy(basis_hbm.at[l], basis.at[l], basis_sem.at[l])
        for l in range(layers)
    ]
    docs_in = [
        pltpu.make_async_copy(
            docs_hbm.at[:, pl.ds(k * part, part)], docs.at[k], docs_sem.at[k]
        )
        for k in range(chunks)
    ]
    for copy in [tests_in, values_in] + basis_in + docs_in:
        copy.start()

    barrier = pltpu.get_barrier_semaphore()

    def greet(i):
        pl.semaphore_signal(
            barrier, inc=1, device_id={"blk": lax.rem(me + 1 + i, n)}, device_id_type=MESH
        )

    repeat(n - 1, greet)

    def copy_of(k, block, slot, target):
        return pltpu.make_async_remote_copy(
            src_ref=ready.at[k, block],
            dst_ref=ready.at[k, block],
            send_sem=send_sem.at[k, slot],
            recv_sem=recv_sem.at[k, block],
            device_id={"blk": target},
            device_id_type=MESH,
        )

    def arrived(k, block):
        copy_of(k, block, block, me).wait_recv()

    def to_core(k, block):
        copy_of(k, block, block + 1 - 2 * c, index(a, b, 1 - c)).start()

    def to_near(k, a_):
        def one(i):
            b_ = lax.rem(b + 1 + i, near)
            copy_of(k, index(a_, b, c), index(a_, b_, c), index(a, b_, c)).start()

        repeat(near - 1, one)

    def send_own(k):
        def one(i):
            a_ = lax.rem(a + 1 + i, far)
            copy_of(k, me, index(a_, b, c), index(a_, b, c)).start()

        repeat(far - 1, one)
        to_near(k, a)
        to_core(k, me)

    def pass_far(k):
        def one(i):
            a_ = lax.rem(a + 1 + i, far)
            arrived(k, index(a_, b, c))
            to_near(k, a_)
            to_core(k, index(a_, b, c))

        repeat(far - 1, one)

    def pass_near(k):
        def outer(j):
            a_ = lax.rem(a + j, far)

            def one(i):
                block = index(a_, lax.rem(b + 1 + i, near), c)
                arrived(k, block)
                to_core(k, block)

            repeat(near - 1, one)

        repeat(far, outer)

    def finish(k):
        repeat(far * near, lambda i: arrived(k, 2 * i + 1 - c))

    def multiply(k):
        docs_in[k].wait()
        doc = docs[k].astype(jnp.bfloat16)

        def one(i):
            rows_at = pl.ds(i * TILE, TILE)
            block = ready[k, pl.ds(i * (TILE // rows), TILE // rows)].reshape(TILE, part)
            product = lax.dot_general(block, doc, NT, preferred_element_type=jnp.float32)
            if k == 0:
                acc[rows_at, :] = product
            else:
                acc[rows_at, :] += product

        repeat(queries // TILE, one)

    tests_in.wait()
    values_in.wait()
    pieces = chunks // layers
    for l in range(layers):
        level = values[l : l + 1, :]
        damping = 0.1 * jnp.mean(level)
        mine = split3(tests[:, l * width : (l + 1) * width])
        basis_in[l].wait()
        turned = jnp.dot(mine, basis[l], preferred_element_type=jnp.float32)
        turned = turned[:rows] + (turned[rows : 2 * rows] + turned[2 * rows :])
        turned = split3(turned / (level + damping))
        for p in range(pieces):
            k = l * pieces + p
            back = lax.dot_general(
                turned, basis[l, p * part : (p + 1) * part, :], NT,
                preferred_element_type=jnp.float32,
            )
            back = back[:rows] + (back[rows : 2 * rows] + back[2 * rows :])
            ready[k, me] = back.astype(jnp.bfloat16)
            if k == 0:
                pl.semaphore_wait(barrier, n - 1)
            send_own(k)

    for step in range(chunks + 2):
        if step < chunks:
            pass_far(step)
        if 1 <= step <= chunks:
            pass_near(step - 1)
        if step >= 2:
            finish(step - 2)
            multiply(step - 2)

    lanes = 128

    def square(i):
        rows_at = pl.ds(i * TILE, TILE)
        raw = acc[rows_at, :]
        raw = raw * raw
        folded = raw[:, :lanes]
        for j in range(1, raw.shape[1] // lanes):
            folded = folded + raw[:, j * lanes : (j + 1) * lanes]
        sums[me, i] = jnp.sum(folded.T, axis=0, keepdims=True)

    repeat(queries // TILE, square)

    def sums_copy(block, slot, target):
        return pltpu.make_async_remote_copy(
            src_ref=sums.at[block],
            dst_ref=sums.at[block],
            send_sem=sums_send.at[slot],
            recv_sem=sums_recv.at[block],
            device_id={"blk": target},
            device_id_type=MESH,
        )

    def tell(i):
        other = lax.rem(me + 1 + i, n)
        sums_copy(me, other, other).start()

    repeat(n - 1, tell)

    def sent(i):
        other = lax.rem(me + 1 + i, n)
        for k in range(chunks):
            copy_of(k, other, other, other).wait_send()

    repeat(n - 1, sent)

    def heard(i):
        other = lax.rem(me + 1 + i, n)
        sums_copy(other, other, other).wait_recv()

    repeat(n - 1, heard)

    def scale(i):
        rows_at = pl.ds(i * TILE, TILE)
        spread = jnp.sum(sums[:, i], axis=0) / total_docs
        factor = 1.0 / jnp.sqrt(spread + 1e-06)
        factor = jnp.broadcast_to(factor, (lanes, TILE)).T
        for j in range(acc.shape[1] // lanes):
            acc[rows_at, j * lanes : (j + 1) * lanes] *= factor
        pltpu.make_async_copy(acc.at[rows_at], out_hbm.at[rows_at], out_sem.at[i]).start()

    repeat(queries // TILE, scale)

    def written(i):
        rows_at = pl.ds(i * TILE, TILE)
        pltpu.make_async_copy(acc.at[rows_at], out_hbm.at[rows_at], out_sem.at[i]).wait()

    repeat(queries // TILE, written)

    def told(i):
        other = lax.rem(me + 1 + i, n)
        sums_copy(me, other, other).wait_send()

    repeat(n - 1, told)


def shards(n, doc_grads, test_grads, eigen_basis, eigen_values):
    docs, columns = doc_grads.shape
    rows = test_grads.shape[0]
    layers, width = eigen_values.shape
    chips = n // 2
    near = 1
    while near * near * 4 <= chips:
        near *= 2
    far = chips // near
    chunks = layers * PIECES
    part = columns // chunks
    queries = n * rows
    anywhere = pl.BlockSpec(memory_space=pl.ANY)
    dma = pltpu.SemaphoreType.DMA
    return pl.pallas_call(
        functools.partial(kernel, far, near),
        out_shape=jax.ShapeDtypeStruct((queries, docs), jnp.float32),
        in_specs=[anywhere] * 4,
        out_specs=anywhere,
        scratch_shapes=[
            pltpu.VMEM((chunks, docs, part), jnp.float32),
            pltpu.VMEM((rows, columns), jnp.float32),
            pltpu.VMEM((layers, width, width), jnp.bfloat16),
            pltpu.VMEM((layers, width), jnp.float32),
            pltpu.VMEM((chunks, n, rows, part), jnp.bfloat16),
            pltpu.VMEM((queries, docs), jnp.float32),
            pltpu.VMEM((n, queries // TILE, 1, TILE), jnp.float32),
            dma((chunks,)),
            dma,
            dma((layers,)),
            dma,
            dma((queries // TILE,)),
            dma((chunks, n)),
            dma((chunks, n)),
            dma((n,)),
            dma((n,)),
        ],
        compiler_params=pltpu.CompilerParams(
            collective_id=0, has_side_effects=True, vmem_limit_bytes=50 * 2**20
        ),
        cost_estimate=pl.CostEstimate(
            flops=2 * queries * docs * columns, bytes_accessed=4 * docs * columns, transcendentals=0
        ),
    )(doc_grads, test_grads, eigen_basis, eigen_values)


def solution(mesh):
    in_specs = (P(("grp", "blk"), None), P(("grp", "blk"), None), P(), P())
    out_specs = P(None, ("grp", "blk"))
    return jax.shard_map(
        functools.partial(shards, mesh.shape["blk"]),
        mesh=mesh, in_specs=in_specs, out_specs=out_specs, check_vma=False,
    )
```

```python
import functools

import jax
import jax.numpy as jnp
from jax import lax
from jax.experimental import pallas as pl
from jax.experimental.pallas import tpu as pltpu
from jax.sharding import PartitionSpec as P

PIECES = 1
DIRECT = 0
TILE = 256
LANES = 128
MESH = pl.DeviceIdType.MESH
NT = (((1,), (1,)), ((), ()))


def repeat(count, body):
    if count <= 16:
        for i in range(count):
            body(i)
    else:
        lax.fori_loop(0, count, lambda i, c: (body(i), c)[1], 0)


def split3(x):
    high = x.astype(jnp.bfloat16)
    rest = x - high.astype(jnp.float32)
    mid = rest.astype(jnp.bfloat16)
    low = (rest - mid.astype(jnp.float32)).astype(jnp.bfloat16)
    return jnp.concatenate([high, mid, low], axis=0)


def kernel(
    docs_hbm, tests_hbm, basis_hbm, values_hbm, raw,
    docs, tests, basis, values, ready, sums,
    docs_sem, tests_sem, basis_sem, values_sem,
    far_send, far_recv, near_send, near_recv, core_send, core_recv,
    sums_send, sums_recv,
):
    layers, width = values.shape
    chunks, _, near, far, rows, part = ready.shape
    n = far * near * 2
    total_docs = n * docs.shape[1]
    queries = n * rows
    tiles = queries // TILE
    me = lax.axis_index("blk")
    c = lax.rem(me, 2)
    b = lax.rem(me // 2, near)
    a = me // (2 * near)

    def index(a_, b_, c_):
        return (a_ * near + b_) * 2 + c_

    def hop(i):
        return far - 1 - i

    def other_far(i):
        return lax.rem(a + hop(i), far)

    def other_near(i):
        return lax.rem(b + 1 + i, near)

    def other(i):
        return lax.rem(me + 1 + i, n)

    tests_in = pltpu.make_async_copy(tests_hbm, tests, tests_sem)
    values_in = pltpu.make_async_copy(values_hbm, values, values_sem)
    basis_in = [
        pltpu.make_async_copy(basis_hbm.at[l], basis.at[l], basis_sem.at[l])
        for l in range(layers)
    ]
    docs_in = [
        pltpu.make_async_copy(
            docs_hbm.at[:, pl.ds(k * part, part)], docs.at[k], docs_sem.at[k]
        )
        for k in range(chunks)
    ]
    for copy in [tests_in, values_in] + basis_in:
        copy.start()

    barrier = pltpu.get_barrier_semaphore()

    def greet(target):
        pl.semaphore_signal(barrier, inc=1, device_id={"blk": target}, device_id_type=MESH)

    repeat(n - 1, lambda i: greet(other(i)))

    def far_copy(k, a_, source):
        return pltpu.make_async_remote_copy(
            src_ref=ready.at[k, c, b, source],
            dst_ref=ready.at[k, c, b, source],
            send_sem=far_send.at[k, a_],
            recv_sem=far_recv.at[k, source],
            device_id={"blk": index(a_, b, c)},
            device_id_type=MESH,
        )

    def near_copy(k, b_, a_, source):
        return pltpu.make_async_remote_copy(
            src_ref=ready.at[k, c, source, a_],
            dst_ref=ready.at[k, c, source, a_],
            send_sem=near_send.at[k, b_, a_],
            recv_sem=near_recv.at[k, source, a_],
            device_id={"blk": index(a, b_, c)},
            device_id_type=MESH,
        )

    def core_copy(k, b_, source):
        return pltpu.make_async_remote_copy(
            src_ref=ready.at[k, source, b_],
            dst_ref=ready.at[k, source, b_],
            send_sem=core_send.at[k, b_],
            recv_sem=core_recv.at[k, b_],
            device_id={"blk": index(a, b, 1 - c)},
            device_id_type=MESH,
        )

    def to_near(k, a_):
        repeat(near - 1, lambda i: near_copy(k, other_near(i), a_, b).start())

    def direct_copy(k, a_, b_):
        return pltpu.make_async_remote_copy(
            src_ref=ready.at[k, c, b, a],
            dst_ref=ready.at[k, c, b, a],
            send_sem=near_send.at[k, b_, a_],
            recv_sem=near_recv.at[k, b, a],
            device_id={"blk": index(a_, b_, c)},
            device_id_type=MESH,
        )

    def send_own(k):
        repeat(far - 1, lambda i: far_copy(k, other_far(i), a).start())
        if k < chunks - DIRECT:
            to_near(k, a)
        else:
            repeat(
                far,
                lambda j: repeat(
                    near - 1,
                    lambda i: direct_copy(k, lax.rem(a + 1 + j, far), other_near(i)).start(),
                ),
            )

    def pass_far(k):
        def one(i):
            a_ = lax.rem(a + far - hop(i), far)
            far_copy(k, a, a_).wait_recv()
            if k < chunks - DIRECT:
                to_near(k, a_)

        repeat(far - 1, one)
        core_copy(k, b, c).start()

    def pass_near(k):
        def one(i):
            b_ = other_near(i)
            repeat(far, lambda j: near_copy(k, b, lax.rem(a + j, far), b_).wait_recv())
            core_copy(k, b_, c).start()

        repeat(near - 1, one)

    def multiply(k):
        repeat(near, lambda i: core_copy(k, i, 1 - c).wait_recv())
        docs_in[k].wait()
        doc = docs[k].astype(jnp.bfloat16)
        blocks = TILE // rows

        def one(i):
            rows_at = pl.ds(i * TILE, TILE)
            parts = []
            for j in range(blocks):
                place = i * blocks + j
                parts.append(ready[k, place % 2, place // 2 % near, place // (2 * near)])
            block = jnp.concatenate(parts, axis=0)
            product = lax.dot_general(block, doc, NT, preferred_element_type=jnp.float32)
            if k > 0:
                product = raw[rows_at, :] + product
            raw[rows_at, :] = product
            if k == chunks - 1:
                square = product * product
                folded = square[:, :LANES]
                for j in range(1, square.shape[1] // LANES):
                    folded = folded + square[:, j * LANES : (j + 1) * LANES]
                sums[me, i] = jnp.sum(folded.T, axis=0, keepdims=True)

        repeat(tiles, one)

    tests_in.wait()
    values_in.wait()
    pieces = chunks // layers
    for l in range(layers):
        level = values[l : l + 1, :]
        damping = 0.1 * jnp.mean(level)
        mine = split3(tests[:, l * width : (l + 1) * width])
        basis_in[l].wait()
        if l == layers - 1:
            for copy in docs_in:
                copy.start()
        turned = jnp.dot(mine, basis[l], preferred_element_type=jnp.float32)
        turned = turned[:rows] + (turned[rows : 2 * rows] + turned[2 * rows :])
        turned = split3(turned / (level + damping))
        for p in range(pieces):
            k = l * pieces + p
            back = lax.dot_general(
                turned, basis[l, p * part : (p + 1) * part, :], NT,
                preferred_element_type=jnp.float32,
            )
            back = back[:rows] + (back[rows : 2 * rows] + back[2 * rows :])
            ready[k, c, b, a] = back.astype(jnp.bfloat16)
            if k == 0:
                pl.semaphore_wait(barrier, n - 1)
            send_own(k)

    for k in range(chunks):
        pass_far(k)
    for k in range(chunks):
        pass_near(k)
        if k > 0:
            multiply(k - 1)
    multiply(chunks - 1)

    def sums_copy(source, target):
        return pltpu.make_async_remote_copy(
            src_ref=sums.at[source],
            dst_ref=sums.at[source],
            send_sem=sums_send.at[target],
            recv_sem=sums_recv.at[source],
            device_id={"blk": target},
            device_id_type=MESH,
        )

    repeat(n - 1, lambda i: sums_copy(me, other(i)).start())

    for k in range(chunks):
        repeat(far - 1, lambda i: far_copy(k, other_far(i), a).wait_send())
        repeat(
            near - 1,
            lambda i: repeat(far, lambda j: near_copy(k, other_near(i), j, b).wait_send()),
        )
        repeat(near, lambda i: core_copy(k, i, c).wait_send())

    repeat(n - 1, lambda i: sums_copy(other(i), other(i)).wait_recv())

    def scale(i):
        rows_at = pl.ds(i * TILE, TILE)
        spread = jnp.sum(sums[:, i], axis=0) / total_docs
        factor = 1.0 / jnp.sqrt(spread + 1e-06)
        factor = jnp.broadcast_to(factor, (LANES, TILE)).T
        for j in range(raw.shape[1] // LANES):
            raw[rows_at, j * LANES : (j + 1) * LANES] *= factor

    repeat(tiles, scale)
    repeat(n - 1, lambda i: sums_copy(me, other(i)).wait_send())


def shards(n, doc_grads, test_grads, eigen_basis, eigen_values):
    docs, columns = doc_grads.shape
    rows = test_grads.shape[0]
    layers, width = eigen_values.shape
    chips = n // 2
    near = 1
    while near * near * 4 <= chips:
        near *= 2
    far = chips // near
    chunks = layers * PIECES
    part = columns // chunks
    queries = n * rows
    tiles = queries // TILE
    hbm = pl.BlockSpec(memory_space=pltpu.HBM)
    dma = pltpu.SemaphoreType.DMA
    return pl.pallas_call(
        kernel,
        out_shape=jax.ShapeDtypeStruct((queries, docs), jnp.float32),
        in_specs=[hbm] * 4,
        out_specs=pl.BlockSpec(memory_space=pltpu.VMEM),
        scratch_shapes=[
            pltpu.VMEM((chunks, docs, part), jnp.float32),
            pltpu.VMEM((rows, columns), jnp.float32),
            pltpu.VMEM((layers, width, width), jnp.bfloat16),
            pltpu.VMEM((layers, width), jnp.float32),
            pltpu.VMEM((chunks, 2, near, far, rows, part), jnp.bfloat16),
            pltpu.VMEM((n, tiles, 1, TILE), jnp.float32),
            dma((chunks,)),
            dma,
            dma((layers,)),
            dma,
            dma((chunks, far)),
            dma((chunks, far)),
            dma((chunks, near, far)),
            dma((chunks, near, far)),
            dma((chunks, near)),
            dma((chunks, near)),
            dma((n,)),
            dma((n,)),
        ],
        compiler_params=pltpu.CompilerParams(
            collective_id=0, has_side_effects=True, vmem_limit_bytes=50 * 2**20
        ),
        cost_estimate=pl.CostEstimate(
            flops=2 * queries * docs * columns, bytes_accessed=4 * docs * columns, transcendentals=0
        ),
    )(*(pltpu.with_memory_space_constraint(x, pltpu.HBM) for x in (doc_grads, test_grads, eigen_basis, eigen_values)))


def solution(mesh):
    in_specs = (P(("grp", "blk"), None), P(("grp", "blk"), None), P(), P())
    out_specs = P(None, ("grp", "blk"))
    return jax.shard_map(
        functools.partial(shards, mesh.shape["blk"]),
        mesh=mesh, in_specs=in_specs, out_specs=out_specs, check_vma=False,
    )
```

```python
import functools

import jax
import jax.numpy as jnp
from jax import lax
from jax.experimental import pallas as pl
from jax.experimental.pallas import tpu as pltpu
from jax.sharding import PartitionSpec as P

PIECES = 1
DIRECT = 0
TILE = 256
LANES = 128
MESH = pl.DeviceIdType.MESH
NT = (((1,), (1,)), ((), ()))


def repeat(count, body):
    if count <= 16:
        for i in range(count):
            body(i)
    else:
        lax.fori_loop(0, count, lambda i, c: (body(i), c)[1], 0)


def split3(x):
    high = x.astype(jnp.bfloat16)
    rest = x - high.astype(jnp.float32)
    mid = rest.astype(jnp.bfloat16)
    low = (rest - mid.astype(jnp.float32)).astype(jnp.bfloat16)
    return jnp.concatenate([high, mid, low], axis=0)


def kernel(
    docs_hbm, tests_hbm, basis_hbm, values_hbm, raw,
    docs, docs16, tests, basis, values, ready, sums,
    docs_sem, tests_sem, basis_sem, values_sem,
    far_send, far_recv, near_send, near_recv, core_send, core_recv,
    sums_send, sums_recv,
):
    layers, width = values.shape
    chunks, _, near, far, rows, part = ready.shape
    n = far * near * 2
    total_docs = n * docs.shape[1]
    queries = n * rows
    tiles = queries // TILE
    me = lax.axis_index("blk")
    c = lax.rem(me, 2)
    b = lax.rem(me // 2, near)
    a = me // (2 * near)

    def index(a_, b_, c_):
        return (a_ * near + b_) * 2 + c_

    def hop(i):
        return far - 1 - i

    def other_far(i):
        return lax.rem(a + hop(i), far)

    def other_near(i):
        return lax.rem(b + 1 + i, near)

    def other(i):
        return lax.rem(me + 1 + i, n)

    tests_in = pltpu.make_async_copy(tests_hbm, tests, tests_sem)
    values_in = pltpu.make_async_copy(values_hbm, values, values_sem)
    basis_in = [
        pltpu.make_async_copy(basis_hbm.at[l], basis.at[l], basis_sem.at[l])
        for l in range(layers)
    ]
    docs_in = [
        pltpu.make_async_copy(
            docs_hbm.at[:, pl.ds(k * part, part)], docs.at[k], docs_sem.at[k]
        )
        for k in range(chunks)
    ]
    for copy in [tests_in, values_in] + basis_in:
        copy.start()

    barrier = pltpu.get_barrier_semaphore()

    def greet(target):
        pl.semaphore_signal(barrier, inc=1, device_id={"blk": target}, device_id_type=MESH)

    repeat(n - 1, lambda i: greet(other(i)))

    def far_copy(k, a_, source):
        return pltpu.make_async_remote_copy(
            src_ref=ready.at[k, c, b, source],
            dst_ref=ready.at[k, c, b, source],
            send_sem=far_send.at[k, a_],
            recv_sem=far_recv.at[k, source],
            device_id={"blk": index(a_, b, c)},
            device_id_type=MESH,
        )

    def near_copy(k, b_, a_, source):
        return pltpu.make_async_remote_copy(
            src_ref=ready.at[k, c, source, a_],
            dst_ref=ready.at[k, c, source, a_],
            send_sem=near_send.at[k, b_, a_],
            recv_sem=near_recv.at[k, source, a_],
            device_id={"blk": index(a, b_, c)},
            device_id_type=MESH,
        )

    def core_copy(k, b_, source):
        return pltpu.make_async_remote_copy(
            src_ref=ready.at[k, source, b_],
            dst_ref=ready.at[k, source, b_],
            send_sem=core_send.at[k, b_],
            recv_sem=core_recv.at[k, b_],
            device_id={"blk": index(a, b, 1 - c)},
            device_id_type=MESH,
        )

    def to_near(k, a_):
        repeat(near - 1, lambda i: near_copy(k, other_near(i), a_, b).start())

    def direct_copy(k, a_, b_):
        return pltpu.make_async_remote_copy(
            src_ref=ready.at[k, c, b, a],
            dst_ref=ready.at[k, c, b, a],
            send_sem=near_send.at[k, b_, a_],
            recv_sem=near_recv.at[k, b, a],
            device_id={"blk": index(a_, b_, c)},
            device_id_type=MESH,
        )

    def send_own(k):
        if k < chunks - DIRECT:
            to_near(k, a)
        repeat(far - 1, lambda i: far_copy(k, other_far(i), a).start())
        if k < chunks - DIRECT:
            return
        if DIRECT:
            repeat(
                far,
                lambda j: repeat(
                    near - 1,
                    lambda i: direct_copy(k, lax.rem(a + 1 + j, far), other_near(i)).start(),
                ),
            )

    def pass_far(k):
        def one(i):
            a_ = lax.rem(a + far - hop(i), far)
            far_copy(k, a, a_).wait_recv()
            if k < chunks - DIRECT:
                to_near(k, a_)

        repeat(far - 1, one)
        core_copy(k, b, c).start()

    def pass_near(k):
        def one(i):
            b_ = other_near(i)
            repeat(far, lambda j: near_copy(k, b, lax.rem(a + j, far), b_).wait_recv())
            core_copy(k, b_, c).start()

        repeat(near - 1, one)

    def multiply(k):
        repeat(near, lambda i: core_copy(k, i, 1 - c).wait_recv())
        doc = docs16[k]
        blocks = TILE // rows

        def one(i):
            rows_at = pl.ds(i * TILE, TILE)
            parts = []
            for j in range(blocks):
                place = i * blocks + j
                parts.append(ready[k, place % 2, place // 2 % near, place // (2 * near)])
            block = jnp.concatenate(parts, axis=0)
            product = lax.dot_general(block, doc, NT, preferred_element_type=jnp.float32)
            if k > 0:
                product = raw[rows_at, :] + product
            raw[rows_at, :] = product
            if k == chunks - 1:
                square = product * product
                folded = square[:, :LANES]
                for j in range(1, square.shape[1] // LANES):
                    folded = folded + square[:, j * LANES : (j + 1) * LANES]
                sums[me, i] = jnp.sum(folded.T, axis=0, keepdims=True)

        repeat(tiles, one)

    tests_in.wait()
    values_in.wait()
    pieces = chunks // layers
    for l in range(layers):
        level = values[l : l + 1, :]
        damping = 0.1 * jnp.mean(level)
        mine = split3(tests[:, l * width : (l + 1) * width])
        basis_in[l].wait()
        if l == layers - 1:
            for copy in docs_in:
                copy.start()
        turned = jnp.dot(mine, basis[l], preferred_element_type=jnp.float32)
        turned = turned[:rows] + (turned[rows : 2 * rows] + turned[2 * rows :])
        turned = split3(turned / (level + damping))
        for p in range(pieces):
            k = l * pieces + p
            back = lax.dot_general(
                turned, basis[l, p * part : (p + 1) * part, :], NT,
                preferred_element_type=jnp.float32,
            )
            back = back[:rows] + (back[rows : 2 * rows] + back[2 * rows :])
            ready[k, c, b, a] = back.astype(jnp.bfloat16)
            if k == 0:
                pl.semaphore_wait(barrier, n - 1)
            send_own(k)

    for k in range(chunks):
        docs_in[k].wait()
        docs16[k] = docs[k].astype(jnp.bfloat16)

    for k in range(chunks):
        pass_far(k)
    for k in range(chunks):
        pass_near(k)
        if k > 0:
            multiply(k - 1)
    multiply(chunks - 1)

    def sums_copy(source, target):
        return pltpu.make_async_remote_copy(
            src_ref=sums.at[source],
            dst_ref=sums.at[source],
            send_sem=sums_send.at[target],
            recv_sem=sums_recv.at[source],
            device_id={"blk": target},
            device_id_type=MESH,
        )

    repeat(n - 1, lambda i: sums_copy(me, other(i)).start())

    for k in range(chunks):
        repeat(far - 1, lambda i: far_copy(k, other_far(i), a).wait_send())
        repeat(
            near - 1,
            lambda i: repeat(far, lambda j: near_copy(k, other_near(i), j, b).wait_send()),
        )
        repeat(near, lambda i: core_copy(k, i, c).wait_send())

    repeat(n - 1, lambda i: sums_copy(other(i), other(i)).wait_recv())

    def scale(i):
        rows_at = pl.ds(i * TILE, TILE)
        spread = jnp.sum(sums[:, i], axis=0) / total_docs
        factor = 1.0 / jnp.sqrt(spread + 1e-06)
        factor = jnp.broadcast_to(factor, (LANES, TILE)).T
        for j in range(raw.shape[1] // LANES):
            raw[rows_at, j * LANES : (j + 1) * LANES] *= factor

    repeat(tiles, scale)
    repeat(n - 1, lambda i: sums_copy(me, other(i)).wait_send())


def shards(n, doc_grads, test_grads, eigen_basis, eigen_values):
    docs, columns = doc_grads.shape
    rows = test_grads.shape[0]
    layers, width = eigen_values.shape
    chips = n // 2
    near = 1
    while near * near * 4 <= chips:
        near *= 2
    far = chips // near
    chunks = layers * PIECES
    part = columns // chunks
    queries = n * rows
    tiles = queries // TILE
    hbm = pl.BlockSpec(memory_space=pltpu.HBM)
    dma = pltpu.SemaphoreType.DMA
    return pl.pallas_call(
        kernel,
        out_shape=jax.ShapeDtypeStruct((queries, docs), jnp.float32),
        in_specs=[hbm] * 4,
        out_specs=pl.BlockSpec(memory_space=pltpu.VMEM),
        scratch_shapes=[
            pltpu.VMEM((chunks, docs, part), jnp.float32),
            pltpu.VMEM((chunks, docs, part), jnp.bfloat16),
            pltpu.VMEM((rows, columns), jnp.float32),
            pltpu.VMEM((layers, width, width), jnp.bfloat16),
            pltpu.VMEM((layers, width), jnp.float32),
            pltpu.VMEM((chunks, 2, near, far, rows, part), jnp.bfloat16),
            pltpu.VMEM((n, tiles, 1, TILE), jnp.float32),
            dma((chunks,)),
            dma,
            dma((layers,)),
            dma,
            dma((chunks, far)),
            dma((chunks, far)),
            dma((chunks, near, far)),
            dma((chunks, near, far)),
            dma((chunks, near)),
            dma((chunks, near)),
            dma((n,)),
            dma((n,)),
        ],
        compiler_params=pltpu.CompilerParams(
            collective_id=0, has_side_effects=True, vmem_limit_bytes=50 * 2**20
        ),
        cost_estimate=pl.CostEstimate(
            flops=2 * queries * docs * columns, bytes_accessed=4 * docs * columns, transcendentals=0
        ),
    )(*(pltpu.with_memory_space_constraint(x, pltpu.HBM) for x in (doc_grads, test_grads, eigen_basis, eigen_values)))


def solution(mesh):
    in_specs = (P(("grp", "blk"), None), P(("grp", "blk"), None), P(), P())
    out_specs = P(None, ("grp", "blk"))
    return jax.shard_map(
        functools.partial(shards, mesh.shape["blk"]),
        mesh=mesh, in_specs=in_specs, out_specs=out_specs, check_vma=False,
    )
```
